256 devices in a mesh: seq: 32 (over z_hi, x, core), ch: 8 (over z_lo, y).
Axes of the slice: x: 4, y: 4, z: 8 (z_hi: 4, z_lo: 2; z = z_hi * 2 + z_lo), core: 2. Of those that a mesh axis runs over, the one named last changes fastest.
Arguments:
- features: bfloat16 [16384, 3, 8192], P('seq', None, 'ch'), may hold values from -6 to 6
- short_w: float32 [3, 3, 8192], P(None, None, 'ch'), may hold values from -3 to 3
- rates: float32 [8192, 16], replicated, may hold values from 1.5258789e-05 to 0.1, as said below
- residues: float32 [8192, 16], replicated, may hold values from -2 to 2
- out_w: bfloat16 [8192, 8192], P('seq', 'ch'), may hold values from -0.0625 to 0.0625
Outputs:
- layer_out: bfloat16 [16384, 8192], P('seq', 'ch')
The draws below stay inside these ranges and needn't reach their ends.
Inputs may be any that keep to these rules, and one draw needn't show every extreme that they name: `rates`: all positive.
All inputs are finite; a program needn't handle non-finite values.
Results may differ from the reference program's by a relative error of at most 0.008.
Values may be sent and summed in bfloat16 or wider, within the bound.
A program may use at most 128 MiB of HBM per device.

```python
import jax
import jax.numpy as jnp
from jax import lax

D = 8192
MODES = 16
SHORT = 3
TOKENS = 16384


def draw_rates(key, part):
    key = jax.random.fold_in(key, 7)
    first = jax.random.fold_in(key, 0)
    lower = 0.25 / TOKENS
    upper = 0.1
    spread = jax.random.uniform(first, (D, MODES), jnp.float32)
    wide = lower * jnp.power(upper / lower, spread)
    return wide


def block_scale(rng, extent, pieces, least, top_value):
    def one(dim, blocks):
        steps = jax.random.uniform(jax.random.fold_in(jax.random.fold_in(rng, 6), dim), (blocks,), jnp.float32, least / len(pieces), top_value / len(pieces))
        return jnp.repeat(jnp.exp(steps), extent[dim] // blocks).reshape((-1,) + (1,) * (len(extent) - dim - 1))

    level = one(*pieces[0])
    for cut in pieces[1:]:
        level = level * one(*cut)
    return level


def centred(rng, shape, scale, reach, shards=(), kind=jnp.bfloat16):
    result = scale * jax.random.normal(rng, shape, jnp.float32)
    if shards:
        result = result * block_scale(rng, shape, shards, -0.22, 0.18)
    return jnp.clip(result, -reach, reach).astype(kind)


def setup_inputs(seed: int = 0) -> dict:
    streams_of = jax.random.split(jax.random.key(seed), 6)
    return {
        "features": centred(streams_of[0], (TOKENS, 3, D), 1.0, 6.0, ((0, 32), (2, 8))),
        "short_w": centred(streams_of[1], (SHORT, 3, D), 0.6, 3.0, ((2, 8),), jnp.float32),
        "rates": draw_rates(jax.random.fold_in(streams_of[5], 71), 0),
        "residues": centred(streams_of[3], (D, MODES), 0.3, 2.0, (), jnp.float32),
        "out_w": centred(streams_of[4], (D, D), D ** -0.5, 0.0625, ((0, 32), (1, 8))),
    }


def short_mix(feat, taps):
    padded = jnp.pad(feat, ((SHORT - 1, 0), (0, 0), (0, 0)))
    total = jnp.zeros_like(feat)
    for j in range(SHORT):
        total = total + taps[j][None] * padded[SHORT - 1 - j:SHORT - 1 - j + TOKENS]
    return total

def modal_filter(rate, resid):
    times = jnp.arange(TOKENS).astype(jnp.float32)

    def add_mode(acc, pair):
        one_rate, one_res = pair
        gain = one_res * jnp.sqrt(2.0 * one_rate)
        return (acc + gain[:, None] * jnp.exp(-one_rate[:, None] * times[None, :]), None)
    start = jnp.zeros((rate.shape[0], TOKENS), jnp.float32)
    filt, _ = lax.scan(add_mode, start, (rate.T, resid.T))
    return filt

def reference(features, short_w, rates, residues, out_w):
    width = D // 8

    def one_block(index):
        begin = (index * width).astype(jnp.int32)
        feat = lax.dynamic_slice_in_dim(features, begin, width, 2).astype(jnp.float32)
        taps = lax.dynamic_slice_in_dim(short_w, begin, width, 2)
        mixed = short_mix(feat, taps)
        query = mixed[:, 0]
        product = lax.optimization_barrier((mixed[:, 1] * mixed[:, 2]).astype(jnp.bfloat16))
        signal = product.astype(jnp.float32).T
        filt = modal_filter(lax.dynamic_slice_in_dim(rates, begin, width, 0), lax.dynamic_slice_in_dim(residues, begin, width, 0))
        spec_u = jnp.fft.rfft(signal, n=2 * TOKENS, axis=-1)
        spec_h = jnp.fft.rfft(filt, n=2 * TOKENS, axis=-1)
        conv = jnp.fft.irfft(spec_u * spec_h, n=2 * TOKENS, axis=-1)[:, :TOKENS]
        conv = lax.optimization_barrier(conv.astype(jnp.bfloat16))
        return (query * conv.astype(jnp.float32).T).astype(jnp.bfloat16)
    blocks = lax.map(one_block, jnp.arange(8, dtype=jnp.int32))
    gated = jnp.transpose(blocks, (1, 0, 2)).reshape(TOKENS, D)
    return jnp.dot(gated, out_w, preferred_element_type=jnp.float32).astype(jnp.bfloat16)
```

```python
import functools

import jax
import jax.numpy as jnp
from jax import lax
from jax.experimental import pallas as pl
from jax.experimental.pallas import tpu as pltpu
from jax.sharding import PartitionSpec as P

MESH = pl.DeviceIdType.MESH
F32 = jnp.float32
BF16 = jnp.bfloat16

BACK = (0, -1, 1, 2)
PARTS = ((0, 160), (160, 160), (320, 96), (416, 96))
LANES = 128
SUB = 8


def layer_kernel(
    f_ref, taps_ref, rate_ref, gain_ref, w_ref, o_ref,
    w_buf, a_buf, acc, q_ref, p_ref, g_ref, v_ref, s_own, s_sib, t_buf, r_buf, h_buf, halo,
    own_sem, halo_sem, x_send, xf_send, z_send, zf_send, d_send, w_recv, d_recv,
    s_sem, t_send, t_recv, r_send, r_recv, h_sem, y_send, yf_send, l_send, a_recv,
):
    toks, width = q_ref.shape
    steps = toks // SUB
    modes = rate_ref.shape[0]
    some = modes // 2
    s = lax.axis_index("seq")
    c = lax.axis_index("ch")
    zh, x, core = s // 8, lax.rem(s // 2, 4), lax.rem(s, 2)
    zl, y = c // 4, lax.rem(c, 4)

    def ring(value, step):
        return lax.rem(value + step + 4, 4)

    def at(dz=0, dx=0, dcore=0, dl=0, dy=0):
        seq = (ring(zh, dz) * 4 + ring(x, dx)) * 2 + lax.rem(core + dcore, 2)
        return (seq, lax.rem(zl + dl, 2) * 4 + ring(y, dy))

    after = (lax.rem(s + 1, 32), c)
    before = (lax.rem(s + 31, 32), c)

    def remote(src, dst, send, recv, device):
        return pltpu.make_async_remote_copy(
            src_ref=src, dst_ref=dst, send_sem=send, recv_sem=recv,
            device_id=device, device_id_type=MESH,
        )

    barrier = pltpu.get_barrier_semaphore()
    partners = [
        at(dcore=1), at(dx=1), at(dx=-1), at(dx=2), at(dz=1), at(dz=-1), at(dz=2),
        at(dl=1), at(dy=1), at(dy=-1), after, before,
    ]
    for device in partners:
        pl.semaphore_signal(barrier, inc=1, device_id=device, device_id_type=MESH)
    pl.semaphore_wait(barrier, len(partners))

    sent = []

    def go(copy):
        copy.start()
        sent.append(copy)

    def w_block(dz, dx):
        return ring(zh, BACK[dz]) * 4 + ring(x, BACK[dx])

    def w_slot(dz, dx, half, of_core):
        rows = pl.ds(pl.multiple_of(of_core * 256 + half * 128, 128), 128)
        return w_buf.at[w_block(dz, dx), rows]

    def w_src(dz, dx, half):
        if dz == 0 and dx == 0:
            return w_ref.at[pl.ds(half * 128, 128)]
        return w_slot(dz, dx, half, core)

    def w_sibling(dz, dx, half):
        go(remote(w_src(dz, dx, half), w_slot(dz, dx, half, core),
                  d_send.at[dz, dx, half], d_recv.at[dz, dx, half], at(dcore=1)))

    def w_x(dz, half):
        for way in (0, 1):
            go(remote(w_src(dz, 0, half), w_slot(dz, 0, half, core),
                      x_send.at[dz, way, half], w_recv.at[dz, 1 + way, half],
                      at(dx=(1, -1)[way])))

    def w_z(half):
        for way in (0, 1):
            go(remote(w_src(0, 0, half), w_slot(0, 0, half, core),
                      z_send.at[way, half], w_recv.at[1 + way, 0, half],
                      at(dz=(1, -1)[way])))

    def w_wait(dz, dx, half):
        slot = w_slot(dz, dx, half, core)
        remote(slot, slot, d_send.at[dz, dx, half], w_recv.at[dz, dx, half], at(dcore=1)).wait_recv()

    def w_wait_sibling(dz, dx, half):
        slot = w_slot(dz, dx, half, 1 - core)
        remote(slot, slot, d_send.at[dz, dx, half], d_recv.at[dz, dx, half], at(dcore=1)).wait_recv()

    def w_from_z(dz, half):
        w_wait(dz, 0, half)
        w_x(dz, half)
        if dz == 1 and half == 0:
            go(remote(w_src(1, 0, 0), w_slot(1, 0, 0, core), zf_send.at[0],
                      w_recv.at[3, 0, 0], at(dz=1)))
        if dz == 2 and half == 1:
            go(remote(w_src(2, 0, 1), w_slot(2, 0, 1, core), zf_send.at[1],
                      w_recv.at[3, 0, 1], at(dz=-1)))
        w_sibling(dz, 0, half)

    def w_from_x(dz, dx, half):
        w_wait(dz, dx, half)
        if dx == 1 and half == 0:
            go(remote(w_src(dz, 1, 0), w_slot(dz, 1, 0, core), xf_send.at[dz, 0],
                      w_recv.at[dz, 3, 0], at(dx=1)))
        if dx == 2 and half == 1:
            go(remote(w_src(dz, 2, 1), w_slot(dz, 2, 1, core), xf_send.at[dz, 1],
                      w_recv.at[dz, 3, 1], at(dx=-1)))
        w_sibling(dz, dx, half)

    def w_x_all(dz):
        for half in (0, 1):
            for dx in (1, 2):
                w_from_x(dz, dx, half)

    def w_x_far(dz):
        for half in (0, 1):
            w_from_x(dz, 3, half)

    def w_whole(dz):
        for dx in range(4):
            for half in (0, 1):
                w_wait_sibling(dz, dx, half)

    go_halo = remote(f_ref.at[:, pl.ds(toks - 16, 16)], halo, halo_sem.at[0], halo_sem.at[1], after)
    go(go_halo)
    for half in (0, 1):
        w_x(0, half)
        w_z(half)
    for half in (0, 1):
        w_sibling(0, 0, half)
    keep = pltpu.make_async_copy(
        w_ref, w_buf.at[w_block(0, 0), pl.ds(pl.multiple_of(core * 256, 256), 256)], own_sem)
    keep.start()

    def lane_group(g):
        return pl.ds(pl.multiple_of(g * LANES, LANES), LANES)

    def mix(cur, back1, back2, taps):
        mixed = [taps[0][k] * cur[k] + taps[1][k] * back1[k] + taps[2][k] * back2[k] for k in range(3)]
        return mixed[0], (mixed[1] * mixed[2]).astype(BF16).astype(F32)

    def load_taps(lanes):
        return [[jnp.broadcast_to(taps_ref[pl.ds(j * 3 + k, 1), lanes], (2 * SUB, LANES))
                 for k in range(3)] for j in range(3)]

    def filter_group(g, carry):
        lanes = lane_group(g)
        taps = load_taps(lanes)

        def pair(m, prev):
            rows = pl.ds(pl.multiple_of(m * 16, 16), 16)
            cur = [f_ref[k, rows, lanes].astype(F32) for k in range(3)]
            back1 = [jnp.concatenate([prev[k][SUB:], cur[k][:SUB]], axis=0) for k in range(3)]
            query, product = mix(cur, back1, prev, taps)
            q_ref[rows, lanes] = query
            p_ref[rows, lanes] = product
            return tuple(cur)

        first = tuple(f_ref[k, pl.ds(0, 16), lanes].astype(F32) for k in range(3))
        lax.fori_loop(1, steps // 2, pair, first, unroll=4)
        return carry

    lax.fori_loop(0, width // LANES, filter_group, 0)
    go_halo.wait_recv()
    top = lax.broadcasted_iota(jnp.int32, (SUB, LANES), 0) == 0
    inner = jnp.where(s > 0, 1.0, 0.0).astype(F32)

    def first_group(g, carry):
        lanes = lane_group(g)
        taps = load_taps(lanes)

        def behind(k, half):
            mine = f_ref[k, pl.ds(toks - 16, 16), lanes].astype(F32)[half * SUB : half * SUB + SUB]
            other = halo[k, :, lanes].astype(F32)[half * SUB : half * SUB + SUB] * inner
            return jnp.where(top, pltpu.roll(other, 1, 0), pltpu.roll(mine, 1, 0))

        cur = [f_ref[k, pl.ds(0, 16), lanes].astype(F32) for k in range(3)]
        late = [behind(k, 1) for k in range(3)]
        back2 = [jnp.concatenate([behind(k, 0), late[k]], axis=0) for k in range(3)]
        back1 = [jnp.concatenate([late[k], cur[k][:SUB]], axis=0) for k in range(3)]
        query, product = mix(cur, back1, back2, taps)
        q_ref[pl.ds(0, 16), lanes] = query
        p_ref[pl.ds(0, 16), lanes] = product
        return carry

    lax.fori_loop(0, width // LANES, first_group, 0)

    place = lax.broadcasted_iota(jnp.int32, (SUB, LANES), 0)

    def shifted(value, n):
        return jnp.where(place >= n, pltpu.roll(value, n, 0), 0.0)

    def state_group(g, carry):
        lanes = lane_group(g)
        rate = [jnp.broadcast_to(rate_ref[pl.ds(r, 1), lanes], (SUB, LANES)) for r in range(modes)]
        decay = [jnp.exp(-rate[r]) for r in range(modes)]

        def step(i, state):
            value = p_ref[pl.ds(pl.multiple_of(i * SUB, SUB), SUB), lanes]
            return tuple(decay[r] * state[r] + value for r in range(modes))

        state = lax.fori_loop(0, steps, step, tuple(jnp.zeros((SUB, LANES), F32) for _ in range(modes)), unroll=8)
        for r in range(modes):
            total = state[r]
            for n in (1, 2, 4):
                total = total + jnp.exp(-rate[r] * float(n * steps)) * shifted(total, n)
            v_ref[pl.ds(r * SUB, SUB), lanes] = total
            s_own[pl.ds(r, 1), lanes] = total[SUB - 1 :]
        return carry

    lax.fori_loop(0, width // LANES, state_group, 0)

    swap = remote(s_own, s_sib, s_sem.at[0], s_sem.at[1], at(dcore=1))
    go(swap)
    w_x_all(0)
    swap.wait_recv()
    mine = pl.ds(pl.multiple_of(core * some, some), some)
    rate_half = rate_ref[mine, :]
    one = jnp.exp(-rate_half * float(toks))
    is_second = core == 1
    lead = jnp.where(is_second, s_sib[mine, :], s_own[mine, :])
    last = jnp.where(is_second, s_own[mine, :], s_sib[mine, :])
    t_buf[0] = one * lead + last
    for k in (1, 2, 3):
        go(remote(t_buf.at[0], t_buf.at[k], t_send.at[k], t_recv.at[k], at(dx=-BACK[k])))
    for k in (1, 2, 3):
        remote(t_buf.at[k], t_buf.at[k], t_send.at[k], t_recv.at[k], at(dcore=1)).wait_recv()

    def prefix(buf, here, unit):
        total = jnp.zeros((some, width), F32)
        for k in (1, 2, 3):
            other = ring(here, BACK[k])
            gap = jnp.maximum(here - 1 - other, 0).astype(F32) * unit
            total = total + jnp.where(other < here, jnp.exp(-rate_half * gap) * buf[k], 0.0)
        return total

    unit = float(2 * toks)
    before_x = prefix(t_buf, x, unit)
    row = jnp.zeros((some, width), F32)
    for k in range(4):
        gap = (3 - ring(x, BACK[k])).astype(F32) * unit
        row = row + jnp.exp(-rate_half * gap) * t_buf[k]
    r_buf[0] = row
    for k in (1, 2, 3):
        go(remote(r_buf.at[0], r_buf.at[k], r_send.at[k], r_recv.at[k], at(dz=-BACK[k])))
    w_from_z(1, 0)
    w_from_z(2, 0)
    for k in (1, 2, 3):
        remote(r_buf.at[k], r_buf.at[k], r_send.at[k], r_recv.at[k], at(dcore=1)).wait_recv()
    h_buf[mine, :] = before_x + jnp.exp(-rate_half * (x.astype(F32) * unit)) * prefix(r_buf, zh, 4 * unit)
    share = remote(h_buf.at[mine], h_buf.at[mine], h_sem.at[0], h_sem.at[1], at(dcore=1))
    go(share)
    w_x_far(0)
    their = pl.ds(pl.multiple_of((1 - core) * some, some), some)
    remote(h_buf.at[their], h_buf.at[their], h_sem.at[0], h_sem.at[1], at(dcore=1)).wait_recv()

    def conv_group(g, carry):
        lanes = lane_group(g)
        decay, gain, state = [], [], []
        for r in range(modes):
            rate = jnp.broadcast_to(rate_ref[pl.ds(r, 1), lanes], (SUB, LANES))
            enter = jnp.broadcast_to(h_buf[pl.ds(r, 1), lanes], (SUB, LANES))
            lead = jnp.broadcast_to(s_sib[pl.ds(r, 1), lanes], (SUB, LANES))
            enter = jnp.where(is_second, jnp.exp(-rate * float(toks)) * enter + lead, enter)
            decay.append(jnp.exp(-rate))
            gain.append(jnp.broadcast_to(gain_ref[pl.ds(r, 1), lanes], (SUB, LANES)))
            ahead = (place * steps).astype(F32)
            state.append(shifted(v_ref[pl.ds(r * SUB, SUB), lanes], 1) + jnp.exp(-rate * ahead) * enter)

        def step(m, state):
            rows = pl.ds(pl.multiple_of(m * 16, 16), 16)
            value, query = p_ref[rows, lanes], q_ref[rows, lanes]
            out = []
            for part in (0, 1):
                now = value[part * SUB : part * SUB + SUB]
                state = tuple(decay[r] * state[r] + now for r in range(modes))
                terms = [gain[r] * state[r] for r in range(modes)]
                while len(terms) > 1:
                    terms = [terms[k] + terms[k + 1] for k in range(0, len(terms), 2)]
                out.append(terms[0])
            conv = jnp.concatenate(out, axis=0).astype(BF16).astype(F32)
            g_ref[rows, lanes] = (query * conv).astype(BF16)
            return state

        lax.fori_loop(0, steps // 2, step, tuple(state), unroll=4)
        return carry

    lax.fori_loop(0, width // LANES, conv_group, 0)

    token = lax.broadcasted_iota(jnp.int32, (toks, toks), 0)
    spot = lax.broadcasted_iota(jnp.int32, (toks, toks), 1)
    order = jnp.where(spot == lax.rem(token, steps) * SUB + token // steps, 1.0, 0.0).astype(BF16)

    def reorder(n, carry):
        cols = pl.ds(pl.multiple_of(n * 256, 256), 256)
        a_buf[c, :, cols] = jnp.dot(order, g_ref[:, cols], preferred_element_type=F32).astype(BF16)
        return carry

    lax.fori_loop(0, width // 256, reorder, 0)

    def a_slot(dl, dy, part):
        first, count = PARTS[part]
        return a_buf.at[lax.rem(zl + dl, 2) * 4 + ring(y, BACK[dy]), pl.ds(first, count)]

    def a_y(dl, part):
        for way in (0, 1):
            go(remote(a_slot(dl, 0, part), a_slot(dl, 0, part), y_send.at[dl, part, way],
                      a_recv.at[dl, 1 + way, part], at(dy=(1, -1)[way])))

    def a_across(dy, part):
        go(remote(a_slot(0, dy, part), a_slot(0, dy, part), l_send.at[dy, part],
                  a_recv.at[1, dy, part], at(dl=1)))

    def a_wait(dl, dy, part):
        slot = a_slot(dl, dy, part)
        remote(slot, slot, l_send.at[dy, part], a_recv.at[dl, dy, part], at(dl=1)).wait_recv()

    def a_on(dl, dy, part):
        way = dy - 1
        go(remote(a_slot(dl, dy, part), a_slot(dl, dy, part), yf_send.at[dl, part],
                  a_recv.at[dl, 3, part], at(dy=(1, -1)[way])))

    def a_near(dl, parts):
        for part in parts:
            for dy in (1, 2):
                a_wait(dl, dy, part)
                if dy - 1 == part % 2:
                    a_on(dl, dy, part)
                if part >= 2:
                    a_across(dy, part)

    def multiply(stage):
        def block(k, carry):
            dz = lax.rem(k // 4 - zh + 4, 4)
            w_rank = jnp.where(dz == 0, 0, jnp.where(dz == 3, 1, jnp.where(dz == 1, 2, 3)))
            ch = k // 2
            dy = lax.rem(lax.rem(ch, 4) - y + 4, 4)
            own = ch // 4 == zl
            a_rank = jnp.where(dy == 0, jnp.where(own, 0, 1), jnp.where(dy == 2, 3, 2))

            @pl.when(jnp.maximum(w_rank, a_rank) == stage)
            def _():
                def tile(n, inner_carry):
                    cols = pl.ds(pl.multiple_of(n * 256, 256), 256)
                    part = pl.ds(pl.multiple_of(lax.rem(k, 2) * 512, 512), 512)
                    acc[:, cols] += jnp.dot(a_buf[ch, :, part], w_buf[k, :, cols],
                                            preferred_element_type=F32)
                    return inner_carry

                lax.fori_loop(0, width // 256, tile, 0)

            return carry

        lax.fori_loop(0, 16, block, 0)

    for part in (2, 3):
        a_y(0, part)
    for part in (0, 1):
        a_across(0, part)
    for part in (2, 3):
        a_across(0, part)
    for part in (0, 1):
        a_y(0, part)
    w_from_z(1, 1)
    w_from_z(2, 1)
    acc[...] = jnp.zeros_like(acc)
    keep.wait()
    a_wait(1, 0, 0)
    a_y(1, 0)
    a_wait(1, 0, 1)
    a_y(1, 1)
    w_whole(0)
    w_x_all(1)
    a_near(0, (2, 3))
    multiply(0)
    w_from_z(3, 0)
    w_from_z(3, 1)
    a_wait(1, 0, 2)
    a_wait(1, 0, 3)
    w_x_far(1)
    w_x_all(2)
    a_near(0, (0, 1))
    w_whole(1)
    multiply(1)
    w_x_far(2)
    w_x_all(3)
    for part in (2, 3):
        a_wait(0, 3, part)
        a_across(3, part)
    a_near(1, (0, 1))
    for part in (2, 3):
        for dy in (1, 2):
            a_wait(1, dy, part)
    w_whole(2)
    multiply(2)
    w_x_far(3)
    for dl in (0, 1):
        for part in range(4):
            if dl == 1 or part < 2:
                a_wait(dl, 3, part)
    w_whole(3)
    multiply(3)
    o_ref[...] = acc[...].astype(BF16)
    for copy in sent:
        copy.wait_send()


def on_device(features, short_w, rates, residues, out_w):
    toks, _, width = features.shape
    taps = short_w.shape[0]
    steps = toks // SUB
    streams = features.reshape(SUB, steps, 3, width).transpose(2, 1, 0, 3).reshape(3, toks, width)
    begin = lax.axis_index("ch") * width
    rate = lax.dynamic_slice_in_dim(rates, begin, width, 0).T
    gain = lax.dynamic_slice_in_dim(residues, begin, width, 0).T * jnp.sqrt(2.0 * rate)
    modes = rate.shape[0]
    dma = pltpu.SemaphoreType.DMA
    vmem = pl.BlockSpec(memory_space=pltpu.VMEM)
    return pl.pallas_call(
        layer_kernel,
        out_shape=jax.ShapeDtypeStruct((toks, width), BF16),
        in_specs=[vmem] * 5,
        out_specs=vmem,
        scratch_shapes=[
            pltpu.VMEM((16, 512, width), BF16),
            pltpu.VMEM((8, toks, width), BF16),
            pltpu.VMEM((toks, width), F32),
            pltpu.VMEM((toks, width), F32),
            pltpu.VMEM((toks, width), F32),
            pltpu.VMEM((toks, width), BF16),
            pltpu.VMEM((modes * SUB, width), F32),
            pltpu.VMEM((modes, width), F32),
            pltpu.VMEM((modes, width), F32),
            pltpu.VMEM((4, modes // 2, width), F32),
            pltpu.VMEM((4, modes // 2, width), F32),
            pltpu.VMEM((modes, width), F32),
            pltpu.VMEM((3, 16, width), BF16),
            dma, dma((2,)),
            dma((4, 2, 2)), dma((4, 2)), dma((2, 2)), dma((2,)), dma((4, 4, 2)), dma((4, 4, 2)), dma((4, 4, 2)),
            dma((2,)), dma((4,)), dma((4,)), dma((4,)), dma((4,)), dma((2,)),
            dma((2, 4, 2)), dma((2, 4)), dma((4, 4)), dma((2, 4, 4)),
        ],
        compiler_params=pltpu.CompilerParams(
            collective_id=0, has_side_effects=True, vmem_limit_bytes=60 * 2**20
        ),
    )(streams, short_w.reshape(taps * 3, width), rate, gain, out_w)


def solution(mesh):
    in_specs = (P("seq", None, "ch"), P(None, None, "ch"), P(), P(), P("seq", "ch"))
    out_specs = P("seq", "ch")
    return jax.shard_map(
        on_device, mesh=mesh, in_specs=in_specs, out_specs=out_specs, check_vma=False
    )
```

```python
import functools

import jax
import jax.numpy as jnp
from jax import lax
from jax.experimental import pallas as pl
from jax.experimental.pallas import tpu as pltpu
from jax.sharding import PartitionSpec as P

MESH = pl.DeviceIdType.MESH
F32 = jnp.float32
BF16 = jnp.bfloat16

BACK = (0, -1, 1, 2)
PARTS = ((0, 176), (176, 176), (352, 80), (432, 80))
LEVELS = ((0, 0), (1, 1), (2, 2), (3, 2), (3, 3), (3, 4))
LANES = 128
SUB = 8


def layer_kernel(
    features_ref, taps_ref, rates_ref, residues_ref, w_ref, o_ref,
    f_ref, w_buf, a_buf, acc, q_ref, p_ref, y_ref, rate_ref, gain_ref, v_ref, s_own, s_sib, t_buf, r_buf, h_buf, halo,
    own_sem, par_sem, feat_sem, halo_sem, x_send, xf_send, z_send, zf_send, d_send, w_recv, d_recv,
    s_sem, t_send, t_recv, r_send, r_recv, h_sem, y_send, yf_send, l_send, a_recv,
):
    toks, width = q_ref.shape
    steps = toks // SUB
    modes = rate_ref.shape[0]
    some = modes // 2
    s = lax.axis_index("seq")
    c = lax.axis_index("ch")
    zh, x, core = s // 8, lax.rem(s // 2, 4), lax.rem(s, 2)
    zl, y = c // 4, lax.rem(c, 4)

    def ring(value, step):
        return lax.rem(value + step + 4, 4)

    def at(dz=0, dx=0, dcore=0, dl=0, dy=0):
        seq = (ring(zh, dz) * 4 + ring(x, dx)) * 2 + lax.rem(core + dcore, 2)
        return (seq, lax.rem(zl + dl, 2) * 4 + ring(y, dy))

    after = (lax.rem(s + 1, 32), c)
    before = (lax.rem(s + 31, 32), c)

    def remote(src, dst, send, recv, device):
        return pltpu.make_async_remote_copy(
            src_ref=src, dst_ref=dst, send_sem=send, recv_sem=recv,
            device_id=device, device_id_type=MESH,
        )

    barrier = pltpu.get_barrier_semaphore()
    partners = [
        at(dcore=1), at(dx=1), at(dx=-1), at(dx=2), at(dz=1), at(dz=-1), at(dz=2),
        at(dl=1), at(dy=1), at(dy=-1), after, before,
    ]
    for device in partners:
        pl.semaphore_signal(barrier, inc=1, device_id=device, device_id_type=MESH)
    params = [
        pltpu.make_async_copy(src.at[:, pl.ds(pl.multiple_of(c * width, width), width)], dst, par_sem.at[k])
        for k, (src, dst) in enumerate(((rates_ref, rate_ref), (residues_ref, gain_ref)))
    ]
    fetch = [pltpu.make_async_copy(features_ref.at[k], f_ref.at[k], feat_sem.at[k]) for k in range(3)]
    for copy in fetch + params:
        copy.start()

    sent = []

    def go(copy):
        copy.start()
        sent.append(copy)

    def w_block(dz, dx):
        return ring(zh, BACK[dz]) * 4 + ring(x, BACK[dx])

    def w_slot(dz, dx, half, of_core):
        block = w_block(dz, dx)
        first = lax.rem(block, 2) * 512 + of_core * 256 + half * 128
        return w_buf.at[block // 2, pl.ds(pl.multiple_of(first, 128), 128)]

    def w_src(dz, dx, half):
        if dz == 0 and dx == 0:
            return w_ref.at[pl.ds(half * 128, 128)]
        return w_slot(dz, dx, half, core)

    def w_sibling(dz, dx, half):
        go(remote(w_src(dz, dx, half), w_slot(dz, dx, half, core),
                  d_send.at[dz, dx, half], d_recv.at[dz, dx, half], at(dcore=1)))

    def w_x(dz, half, ways=(0, 1)):
        for way in ways:
            go(remote(w_src(dz, 0, half), w_slot(dz, 0, half, core),
                      x_send.at[dz, way, half], w_recv.at[dz, 1 + way, half],
                      at(dx=(1, -1)[way])))

    def w_z(half, ways=(0, 1)):
        for way in ways:
            go(remote(w_src(0, 0, half), w_slot(0, 0, half, core),
                      z_send.at[way, half], w_recv.at[1 + way, 0, half],
                      at(dz=(1, -1)[way])))

    def w_wait(dz, dx, half):
        slot = w_slot(dz, dx, half, core)
        remote(slot, slot, d_send.at[dz, dx, half], w_recv.at[dz, dx, half], at(dcore=1)).wait_recv()

    def w_wait_sibling(dz, dx, half):
        slot = w_slot(dz, dx, half, 1 - core)
        remote(slot, slot, d_send.at[dz, dx, half], d_recv.at[dz, dx, half], at(dcore=1)).wait_recv()

    def w_from_z(dz, half):
        w_wait(dz, 0, half)
        if dz < 3:
            w_x(dz, half)
        if dz == 1 and half == 0:
            go(remote(w_src(1, 0, 0), w_slot(1, 0, 0, core), zf_send.at[0],
                      w_recv.at[3, 0, 0], at(dz=1)))
        if dz == 2 and half == 1:
            go(remote(w_src(2, 0, 1), w_slot(2, 0, 1, core), zf_send.at[1],
                      w_recv.at[3, 0, 1], at(dz=-1)))
        w_sibling(dz, 0, half)

    def w_from_x(dz, dx, half):
        w_wait(dz, dx, half)
        if dx == 1 and half == 0:
            go(remote(w_src(dz, 1, 0), w_slot(dz, 1, 0, core), xf_send.at[dz, 0],
                      w_recv.at[dz, 3, 0], at(dx=1)))
        if dx == 2 and half == 1:
            go(remote(w_src(dz, 2, 1), w_slot(dz, 2, 1, core), xf_send.at[dz, 1],
                      w_recv.at[dz, 3, 1], at(dx=-1)))
        w_sibling(dz, dx, half)

    def w_x_far(dz):
        for half in (0, 1):
            w_from_x(dz, 3, half)

    def w_whole(dz):
        for dx in range(4):
            for half in (0, 1):
                w_wait_sibling(dz, dx, half)

    place = lax.broadcasted_iota(jnp.int32, (SUB, LANES), 0)

    def lane_group(g):
        return pl.ds(pl.multiple_of(g * LANES, LANES), LANES)

    def load_taps(lanes):
        return [[jnp.broadcast_to(taps_ref[j, pl.ds(k, 1), lanes], (SUB, LANES))
                 for k in range(3)] for j in range(3)]

    def filter_rows(g, lanes, taps, m, prev):
        rows = pl.ds(pl.multiple_of(m * 16, 16), 16)
        cur = [f_ref[k, rows, lanes].astype(F32) for k in range(3)]
        query, product = [], []
        for half in (0, 1):
            mixed, later = [], []
            for k in range(3):
                now = cur[k][half * SUB : half * SUB + SUB]
                one, two = pltpu.roll(now, 1, 0), pltpu.roll(now, 2, 0)
                back1 = jnp.where(place < 1, prev[k][0], one)
                back2 = jnp.where(place < 2, prev[k][1], two)
                mixed.append(taps[0][k] * now + taps[1][k] * back1 + taps[2][k] * back2)
                later.append((one, two))
            prev = later
            query.append(mixed[0])
            product.append(mixed[1] * mixed[2])
        q_ref[rows, lanes] = jnp.concatenate(query, axis=0)
        p_ref[g, rows, :] = jnp.concatenate(product, axis=0).astype(BF16).astype(F32)
        return prev

    def rolled(block):
        end = block[SUB:]
        return (pltpu.roll(end, 1, 0), pltpu.roll(end, 2, 0))

    def filter_group(g, carry):
        lanes = lane_group(g)
        taps = load_taps(lanes)
        first = [(jnp.zeros((SUB, LANES), F32),) * 2 for k in range(3)]
        lax.fori_loop(0, toks // 16, lambda m, prev: filter_rows(g, lanes, taps, m, prev), first, unroll=4)
        return carry

    groups = width // LANES
    for copy in fetch:
        copy.wait()
    lax.fori_loop(0, groups, filter_group, 0)
    pl.semaphore_wait(barrier, len(partners))
    go_halo = remote(f_ref.at[:, pl.ds(toks - 16, 16)], halo, halo_sem.at[0], halo_sem.at[1], after)
    go(go_halo)
    for way in (0, 1):
        w_x(0, way, (way,))
        w_z(way, (way,))
    for way in (0, 1):
        w_x(0, 1 - way, (way,))
    for half in (0, 1):
        w_sibling(0, 0, half)
    mine_at = pl.multiple_of(lax.rem(w_block(0, 0), 2) * 512 + core * 256, 256)
    keep = pltpu.make_async_copy(w_ref, w_buf.at[w_block(0, 0) // 2, pl.ds(mine_at, 256)], own_sem)
    keep.start()
    for copy in params:
        copy.wait()
    gain_ref[...] = gain_ref[...] * jnp.sqrt(2.0 * rate_ref[...])

    def shifted(value, n):
        return jnp.where(place >= n, pltpu.roll(value, n, 0), 0.0)

    def row_of(ref, r, lanes):
        return jnp.broadcast_to(ref[pl.ds(r, 1), lanes], (SUB, LANES))

    def state_group(g, carry):
        lanes = lane_group(g)
        rate = [row_of(rate_ref, r, lanes) for r in range(modes)]
        decay = [jnp.exp(-rate[r]) for r in range(modes)]

        def step(i, state):
            value = p_ref[g, pl.ds(i, SUB, stride=steps), :]
            return tuple(decay[r] * state[r] + value for r in range(modes))

        state = lax.fori_loop(0, steps, step, tuple(jnp.zeros((SUB, LANES), F32) for _ in range(modes)), unroll=8)
        for r in range(modes):
            v_ref[pl.ds(r * SUB, SUB), lanes] = state[r]
        return carry

    lax.fori_loop(0, groups, state_group, 0)

    go_halo.wait_recv()
    inner = jnp.where(s > 0, 1.0, 0.0).astype(F32)

    def first_group(g, carry):
        lanes = lane_group(g)
        prev = [rolled(halo[k, :, lanes].astype(F32) * inner) for k in range(3)]
        old = p_ref[g, pl.ds(0, SUB), :]
        filter_rows(g, lanes, load_taps(lanes), 0, prev)
        change = p_ref[g, pl.ds(0, SUB), :] - old
        change = [jnp.broadcast_to(change[k : k + 1], (SUB, LANES)) for k in (0, 1)]
        for r in range(modes):
            rate = row_of(rate_ref, r, lanes)
            far = jnp.exp(-rate * float(steps - 2))
            enter = far * (change[1] + jnp.exp(-rate) * change[0])
            total = v_ref[pl.ds(r * SUB, SUB), lanes] + jnp.where(place < 1, enter, 0.0)
            for n in (1, 2, 4):
                total = total + jnp.exp(-rate * float(n * steps)) * shifted(total, n)
            v_ref[pl.ds(r * SUB, SUB), lanes] = total
            s_own[pl.ds(r, 1), lanes] = total[SUB - 1 :]
        return carry

    lax.fori_loop(0, groups, first_group, 0)

    def conv_group(g, carry):
        lanes = lane_group(g)
        decay = [jnp.exp(-row_of(rate_ref, r, lanes)) for r in range(modes)]
        gain = [row_of(gain_ref, r, lanes) for r in range(modes)]
        enter = tuple(shifted(v_ref[pl.ds(r * SUB, SUB), lanes], 1) for r in range(modes))

        def step(i, state):
            at_step = pl.ds(i, SUB, stride=steps)
            value = p_ref[g, at_step, :]
            state = tuple(decay[r] * state[r] + value for r in range(modes))
            y_ref[g, at_step, :] = tree([gain[r] * state[r] for r in range(modes)])
            return state

        lax.fori_loop(0, steps, step, enter, unroll=8)
        return carry

    def tree(terms):
        while len(terms) > 1:
            terms = [terms[k] + terms[k + 1] for k in range(0, len(terms), 2)]
        return terms[0]

    swap = remote(s_own, s_sib, s_sem.at[0], s_sem.at[1], at(dcore=1))
    go(swap)
    lax.fori_loop(0, 1, conv_group, 0)
    swap.wait_recv()
    mine = pl.ds(pl.multiple_of(core * some, some), some)
    rate_half = rate_ref[mine, :]
    one = jnp.exp(-rate_half * float(toks))
    is_second = core == 1
    lead = jnp.where(is_second, s_sib[mine, :], s_own[mine, :])
    last = jnp.where(is_second, s_own[mine, :], s_sib[mine, :])
    t_buf[0] = one * lead + last
    for k in (1, 2, 3):
        go(remote(t_buf.at[0], t_buf.at[k], t_send.at[k], t_recv.at[k], at(dx=-BACK[k])))
    lax.fori_loop(1, 4, conv_group, 0)
    for k in (1, 2, 3):
        remote(t_buf.at[k], t_buf.at[k], t_send.at[k], t_recv.at[k], at(dcore=1)).wait_recv()

    unit = float(2 * toks)
    row = jnp.zeros((some, width), F32)
    for k in range(4):
        gap = (3 - ring(x, BACK[k])).astype(F32) * unit
        row = row + jnp.exp(-rate_half * gap) * t_buf[k]
    r_buf[0] = row
    onward = []
    for k in (1, 2, 3):
        copy = remote(r_buf.at[0], r_buf.at[k], r_send.at[k], r_recv.at[k], at(dz=-BACK[k]))
        later = ring(zh, -BACK[k]) > zh
        pl.when(later)(copy.start)
        onward.append((later, copy))
    w_from_z(1, 0)
    w_z(0, (1,))
    total = jnp.zeros((some, width), F32)
    for k in (1, 2, 3):
        other = ring(x, BACK[k])
        gap = jnp.maximum(x - 1 - other, 0).astype(F32) * unit
        total = total + jnp.where(other < x, jnp.exp(-rate_half * gap) * t_buf[k], 0.0)
    h_buf[mine, :] = total
    lax.fori_loop(4, 7, conv_group, 0)
    for k in (1, 2, 3):
        other = ring(zh, BACK[k])

        @pl.when(other < zh)
        def _():
            remote(r_buf.at[k], r_buf.at[k], r_send.at[k], r_recv.at[k], at(dcore=1)).wait_recv()
            gap = (4 * (zh - 1 - other) + x).astype(F32) * unit
            h_buf[mine, :] += jnp.exp(-rate_half * gap) * r_buf[k]

    share = remote(h_buf.at[mine], h_buf.at[mine], h_sem.at[0], h_sem.at[1], at(dcore=1))
    go(share)
    w_from_x(0, 1, 0)
    w_from_x(0, 2, 0)
    w_from_z(2, 1)
    lax.fori_loop(7, 8, conv_group, 0)
    their = pl.ds(pl.multiple_of((1 - core) * some, some), some)
    remote(h_buf.at[their], h_buf.at[their], h_sem.at[0], h_sem.at[1], at(dcore=1)).wait_recv()

    def gate_group(g, carry):
        lanes = lane_group(g)
        decay, state = [], []
        for r in range(modes):
            rate = row_of(rate_ref, r, lanes)
            enter = row_of(h_buf, r, lanes)
            enter = jnp.where(is_second, jnp.exp(-rate * float(toks)) * enter + row_of(s_sib, r, lanes), enter)
            decay.append(jnp.exp(-rate * float(SUB)))
            state.append(row_of(gain_ref, r, lanes) * jnp.exp(-rate * (place + 1).astype(F32)) * enter)

        def step(m, state):
            rows = pl.ds(pl.multiple_of(m * 16, 16), 16)
            added = []
            for _ in (0, 1):
                added.append(tree(list(state)))
                state = tuple(decay[r] * state[r] for r in range(modes))
            conv = (y_ref[g, rows, :] + jnp.concatenate(added, axis=0)).astype(BF16).astype(F32)
            a_buf[c, rows, lanes] = (q_ref[rows, lanes] * conv).astype(BF16)
            return state

        lax.fori_loop(0, toks // 16, step, tuple(state), unroll=4)
        return carry

    lax.fori_loop(0, groups, gate_group, 0)

    def a_slot(dl, dy, part):
        first, count = PARTS[part]
        return a_buf.at[lax.rem(zl + dl, 2) * 4 + ring(y, BACK[dy]), pl.ds(first, count)]

    def a_y(dl, part):
        for way in (0, 1):
            go(remote(a_slot(dl, 0, part), a_slot(dl, 0, part), y_send.at[dl, part, way],
                      a_recv.at[dl, 1 + way, part], at(dy=(1, -1)[way])))

    def a_across(dy, part):
        go(remote(a_slot(0, dy, part), a_slot(0, dy, part), l_send.at[dy, part],
                  a_recv.at[1, dy, part], at(dl=1)))

    def a_wait(dl, dy, part):
        slot = a_slot(dl, dy, part)
        remote(slot, slot, l_send.at[dy, part], a_recv.at[dl, dy, part], at(dl=1)).wait_recv()

    def a_on(dl, dy, part):
        way = dy - 1
        go(remote(a_slot(dl, dy, part), a_slot(dl, dy, part), yf_send.at[dl, part],
                  a_recv.at[dl, 3, part], at(dy=(1, -1)[way])))

    def a_near(dl, part, dy):
        a_wait(dl, dy, part)
        if dy - 1 == part % 2:
            a_on(dl, dy, part)

    def multiply(stage):
        def ready(w_rank, a_rank, level):
            return jnp.logical_and(w_rank <= LEVELS[level][0], a_rank <= LEVELS[level][1])

        def block(ch, carry):
            dz = lax.rem(ch // 2 - zh + 4, 4)
            w_rank = jnp.where(dz == 0, 0, jnp.where(dz == 3, 1, jnp.where(dz == 1, 2, 3)))
            dy = lax.rem(lax.rem(ch, 4) - y + 4, 4)
            own = ch // 4 == zl
            a_rank = jnp.where(dy == 0, jnp.where(own, 0, 1), jnp.where(dy == 2, jnp.where(own, 3, 4), 2))
            now = ready(w_rank, a_rank, stage)
            if stage:
                now = jnp.logical_and(now, jnp.logical_not(ready(w_rank, a_rank, stage - 1)))

            @pl.when(now)
            def _():
                for n in range(0, width, 256):
                    acc[:, n : n + 256] += jnp.dot(a_buf[ch], w_buf[ch, :, n : n + 256],
                                                   preferred_element_type=F32)

            return carry

        lax.fori_loop(0, 8, block, 0)

    acc[...] = jnp.zeros_like(acc)
    keep.wait()
    w_from_x(0, 1, 1)
    a_y(0, 0)
    a_y(0, 3)
    a_across(0, 1)
    a_y(0, 2)
    w_from_x(2, 2, 1)
    w_from_x(0, 2, 1)
    w_z(1, (0,))
    w_from_x(1, 1, 0)
    a_near(0, 2, 2)
    a_y(0, 1)
    a_across(2, 2)
    w_from_z(3, 0)
    w_from_z(2, 0)
    w_from_x(2, 1, 0)
    w_x(3, 0, (1,))
    w_from_z(3, 1)
    a_wait(1, 0, 1)
    a_y(1, 1)
    w_from_x(2, 3, 1)
    a_across(0, 0)
    a_near(0, 1, 2)
    w_from_x(0, 3, 0)
    w_from_x(1, 2, 0)
    w_x(3, 1, (1,))
    a_near(0, 3, 1)
    a_near(0, 2, 1)
    w_from_x(0, 3, 1)
    w_x(3, 1, (0,))
    w_from_x(2, 3, 0)
    a_wait(1, 2, 2)
    a_near(0, 0, 2)
    w_from_z(1, 1)
    a_near(0, 0, 1)
    w_from_x(3, 1, 1)
    w_from_x(3, 2, 0)
    a_across(0, 2)
    a_across(0, 3)
    w_from_x(1, 3, 0)
    w_whole(0)
    w_x(3, 0, (0,))
    a_across(1, 2)
    w_from_x(2, 2, 0)
    a_near(0, 3, 2)
    a_wait(1, 0, 0)
    a_y(1, 0)
    a_across(1, 3)
    w_from_x(1, 2, 1)
    w_from_x(1, 1, 1)
    a_near(0, 1, 1)
    w_from_x(2, 1, 1)
    multiply(0)
    w_from_x(3, 1, 0)
    a_across(2, 3)
    a_near(1, 1, 1)
    w_from_x(3, 2, 1)
    a_wait(1, 0, 2)
    w_from_x(1, 3, 1)
    a_near(1, 1, 2)
    a_near(1, 0, 2)
    w_whole(1)
    a_near(1, 0, 1)
    w_from_x(3, 3, 1)
    a_wait(0, 3, 3)
    a_across(3, 3)
    a_wait(1, 1, 3)
    a_wait(1, 0, 3)
    multiply(1)
    a_wait(1, 2, 3)
    w_from_x(3, 3, 0)
    w_whole(2)
    a_wait(0, 3, 0)
    a_wait(1, 1, 2)
    a_wait(0, 3, 2)
    a_across(3, 2)
    a_wait(0, 3, 1)
    multiply(2)
    w_whole(3)
    multiply(3)
    a_wait(1, 3, 1)
    a_wait(1, 3, 0)
    a_wait(1, 3, 2)
    a_wait(1, 3, 3)
    multiply(4)
    multiply(5)
    o_ref[...] = acc[...].astype(BF16)
    for copy in sent:
        copy.wait_send()
    for later, copy in onward:
        pl.when(later)(copy.wait_send)


def on_device(features, short_w, rates, residues, out_w):
    toks, _, width = features.shape
    modes = rates.shape[1]
    dma = pltpu.SemaphoreType.DMA
    vmem = pl.BlockSpec(memory_space=pltpu.VMEM)
    hbm = pl.BlockSpec(memory_space=pl.ANY)
    return pl.pallas_call(
        layer_kernel,
        out_shape=jax.ShapeDtypeStruct((toks, width), BF16),
        in_specs=[hbm, vmem, hbm, hbm, hbm],
        out_specs=vmem,
        scratch_shapes=[
            pltpu.VMEM((3, toks, width), BF16),
            pltpu.VMEM((8, 1024, width), BF16),
            pltpu.VMEM((8, toks, width), BF16),
            pltpu.VMEM((toks, width), F32),
            pltpu.VMEM((toks, width), F32),
            pltpu.VMEM((width // LANES, toks, LANES), F32),
            pltpu.VMEM((width // LANES, toks, LANES), F32),
            pltpu.VMEM((modes, width), F32),
            pltpu.VMEM((modes, width), F32),
            pltpu.VMEM((modes * SUB, width), F32),
            pltpu.VMEM((modes, width), F32),
            pltpu.VMEM((modes, width), F32),
            pltpu.VMEM((4, modes // 2, width), F32),
            pltpu.VMEM((4, modes // 2, width), F32),
            pltpu.VMEM((modes, width), F32),
            pltpu.VMEM((3, 16, width), BF16),
            dma, dma((2,)), dma((3,)), dma((2,)),
            dma((4, 2, 2)), dma((4, 2)), dma((2, 2)), dma((2,)), dma((4, 4, 2)), dma((4, 4, 2)), dma((4, 4, 2)),
            dma((2,)), dma((4,)), dma((4,)), dma((4,)), dma((4,)), dma((2,)),
            dma((2, 4, 2)), dma((2, 4)), dma((4, 4)), dma((2, 4, 4)),
        ],
        compiler_params=pltpu.CompilerParams(
            collective_id=0, has_side_effects=True, vmem_limit_bytes=60 * 2**20
        ),
    )(features.transpose(1, 0, 2), short_w, rates.T, residues.T, out_w)


def solution(mesh):
    in_specs = (P("seq", None, "ch"), P(None, None, "ch"), P(), P(), P("seq", "ch"))
    out_specs = P("seq", "ch")
    return jax.shard_map(
        on_device, mesh=mesh, in_specs=in_specs, out_specs=out_specs, check_vma=False
    )
```

```python
import functools

import jax
import jax.numpy as jnp
from jax import lax
from jax.experimental import pallas as pl
from jax.experimental.pallas import tpu as pltpu
from jax.sharding import PartitionSpec as P

MESH = pl.DeviceIdType.MESH
F32 = jnp.float32
BF16 = jnp.bfloat16

BACK = (0, -1, 1, 2)
PARTS = ((0, 176), (176, 176), (352, 80), (432, 80))
LEVELS = ((0, 0), (1, 1), (2, 2), (3, 2), (3, 3), (3, 4))
LANES = 128
SUB = 8


def layer_kernel(
    features_ref, taps_ref, rates_ref, residues_ref, w_ref, o_ref,
    f_ref, w_buf, a_buf, acc, q_ref, p_ref, y_ref, rate_ref, gain_ref, v_ref, s_own, s_sib, t_buf, r_buf, h_buf, halo,
    own_sem, par_sem, feat_sem, halo_sem, x_send, xf_send, z_send, zf_send, d_send, w_recv, d_recv,
    s_sem, t_send, t_recv, r_send, r_recv, h_sem, y_send, yf_send, l_send, a_recv,
):
    toks, width = q_ref.shape
    steps = toks // SUB
    modes = rate_ref.shape[0]
    some = modes // 2
    s = lax.axis_index("seq")
    c = lax.axis_index("ch")
    zh, x, core = s // 8, lax.rem(s // 2, 4), lax.rem(s, 2)
    zl, y = c // 4, lax.rem(c, 4)

    def ring(value, step):
        return lax.rem(value + step + 4, 4)

    def at(dz=0, dx=0, dcore=0, dl=0, dy=0):
        seq = (ring(zh, dz) * 4 + ring(x, dx)) * 2 + lax.rem(core + dcore, 2)
        return (seq, lax.rem(zl + dl, 2) * 4 + ring(y, dy))

    after = (lax.rem(s + 1, 32), c)
    before = (lax.rem(s + 31, 32), c)

    def remote(src, dst, send, recv, device):
        return pltpu.make_async_remote_copy(
            src_ref=src, dst_ref=dst, send_sem=send, recv_sem=recv,
            device_id=device, device_id_type=MESH,
        )

    barrier = pltpu.get_barrier_semaphore()
    partners = [
        at(dcore=1), at(dx=1), at(dx=-1), at(dx=2), at(dz=1), at(dz=-1), at(dz=2),
        at(dl=1), at(dy=1), at(dy=-1), after, before,
    ]
    for device in partners:
        pl.semaphore_signal(barrier, inc=1, device_id=device, device_id_type=MESH)
    params = [
        pltpu.make_async_copy(src.at[:, pl.ds(pl.multiple_of(c * width, width), width)], dst, par_sem.at[k])
        for k, (src, dst) in enumerate(((rates_ref, rate_ref), (residues_ref, gain_ref)))
    ]
    fetch = [pltpu.make_async_copy(features_ref.at[k], f_ref.at[k], feat_sem.at[k]) for k in range(3)]
    for copy in fetch + params:
        copy.start()

    sent = []

    def go(copy):
        copy.start()
        sent.append(copy)

    def w_block(dz, dx):
        return ring(zh, BACK[dz]) * 4 + ring(x, BACK[dx])

    def w_slot(dz, dx, half, of_core):
        block = w_block(dz, dx)
        first = lax.rem(block, 2) * 512 + of_core * 256 + half * 128
        return w_buf.at[block // 2, pl.ds(pl.multiple_of(first, 128), 128)]

    def w_src(dz, dx, half):
        if dz == 0 and dx == 0:
            return w_ref.at[pl.ds(half * 128, 128)]
        return w_slot(dz, dx, half, core)

    def w_sibling(dz, dx, half):
        go(remote(w_src(dz, dx, half), w_slot(dz, dx, half, core),
                  d_send.at[dz, dx, half], d_recv.at[dz, dx, half], at(dcore=1)))

    def w_x(dz, half, ways=(0, 1)):
        for way in ways:
            go(remote(w_src(dz, 0, half), w_slot(dz, 0, half, core),
                      x_send.at[dz, way, half], w_recv.at[dz, 1 + way, half],
                      at(dx=(1, -1)[way])))

    def w_z(half, ways=(0, 1)):
        for way in ways:
            go(remote(w_src(0, 0, half), w_slot(0, 0, half, core),
                      z_send.at[way, half], w_recv.at[1 + way, 0, half],
                      at(dz=(1, -1)[way])))

    def w_wait(dz, dx, half):
        slot = w_slot(dz, dx, half, core)
        remote(slot, slot, d_send.at[dz, dx, half], w_recv.at[dz, dx, half], at(dcore=1)).wait_recv()

    def w_wait_sibling(dz, dx, half):
        slot = w_slot(dz, dx, half, 1 - core)
        remote(slot, slot, d_send.at[dz, dx, half], d_recv.at[dz, dx, half], at(dcore=1)).wait_recv()

    def w_from_z(dz, half):
        w_wait(dz, 0, half)
        if dz < 3:
            w_x(dz, half)
        if dz == 1 and half == 0:
            go(remote(w_src(1, 0, 0), w_slot(1, 0, 0, core), zf_send.at[0],
                      w_recv.at[3, 0, 0], at(dz=1)))
        if dz == 2 and half == 1:
            go(remote(w_src(2, 0, 1), w_slot(2, 0, 1, core), zf_send.at[1],
                      w_recv.at[3, 0, 1], at(dz=-1)))
        w_sibling(dz, 0, half)

    def w_from_x(dz, dx, half):
        w_wait(dz, dx, half)
        if dx == 1 and half == 0:
            go(remote(w_src(dz, 1, 0), w_slot(dz, 1, 0, core), xf_send.at[dz, 0],
                      w_recv.at[dz, 3, 0], at(dx=1)))
        if dx == 2 and half == 1:
            go(remote(w_src(dz, 2, 1), w_slot(dz, 2, 1, core), xf_send.at[dz, 1],
                      w_recv.at[dz, 3, 1], at(dx=-1)))
        w_sibling(dz, dx, half)

    def w_x_far(dz):
        for half in (0, 1):
            w_from_x(dz, 3, half)

    def w_whole(dz):
        for dx in range(4):
            for half in (0, 1):
                w_wait_sibling(dz, dx, half)

    place = lax.broadcasted_iota(jnp.int32, (SUB, LANES), 0)

    def lane_group(g):
        return pl.ds(pl.multiple_of(g * LANES, LANES), LANES)

    def load_taps(lanes):
        return [[jnp.broadcast_to(taps_ref[j, pl.ds(k, 1), lanes], (SUB, LANES))
                 for k in range(3)] for j in range(3)]

    def filter_rows(g, lanes, taps, m, prev):
        rows = pl.ds(pl.multiple_of(m * 16, 16), 16)
        cur = [f_ref[k, rows, lanes].astype(F32) for k in range(3)]
        query, product = [], []
        for half in (0, 1):
            mixed, later = [], []
            for k in range(3):
                now = cur[k][half * SUB : half * SUB + SUB]
                one, two = pltpu.roll(now, 1, 0), pltpu.roll(now, 2, 0)
                back1 = jnp.where(place < 1, prev[k][0], one)
                back2 = jnp.where(place < 2, prev[k][1], two)
                mixed.append(taps[0][k] * now + taps[1][k] * back1 + taps[2][k] * back2)
                later.append((one, two))
            prev = later
            query.append(mixed[0])
            product.append(mixed[1] * mixed[2])
        q_ref[rows, lanes] = jnp.concatenate(query, axis=0)
        p_ref[g, rows, :] = jnp.concatenate(product, axis=0).astype(BF16).astype(F32)
        return prev

    def rolled(block):
        end = block[SUB:]
        return (pltpu.roll(end, 1, 0), pltpu.roll(end, 2, 0))

    def filter_group(g, carry):
        lanes = lane_group(g)
        taps = load_taps(lanes)
        first = [(jnp.zeros((SUB, LANES), F32),) * 2 for k in range(3)]
        lax.fori_loop(0, toks // 16, lambda m, prev: filter_rows(g, lanes, taps, m, prev), first, unroll=4)
        return carry

    groups = width // LANES
    for copy in fetch:
        copy.wait()
    lax.fori_loop(0, groups, filter_group, 0)
    pl.semaphore_wait(barrier, len(partners))
    go_halo = remote(f_ref.at[:, pl.ds(toks - 16, 16)], halo, halo_sem.at[0], halo_sem.at[1], after)
    go(go_halo)
    for way in (0, 1):
        w_x(0, way, (way,))
        w_z(way, (way,))
    for way in (0, 1):
        w_x(0, 1 - way, (way,))
    for half in (0, 1):
        w_sibling(0, 0, half)
    mine_at = pl.multiple_of(lax.rem(w_block(0, 0), 2) * 512 + core * 256, 256)
    keep = pltpu.make_async_copy(w_ref, w_buf.at[w_block(0, 0) // 2, pl.ds(mine_at, 256)], own_sem)
    keep.start()
    for copy in params:
        copy.wait()
    gain_ref[...] = gain_ref[...] * jnp.sqrt(2.0 * rate_ref[...])

    def shifted(value, n):
        return jnp.where(place >= n, pltpu.roll(value, n, 0), 0.0)

    def row_of(ref, r, lanes):
        return jnp.broadcast_to(ref[pl.ds(r, 1), lanes], (SUB, LANES))

    def state_group(g, carry):
        lanes = lane_group(g)
        rate = [row_of(rate_ref, r, lanes) for r in range(modes)]
        decay = [jnp.exp(-rate[r]) for r in range(modes)]

        def step(i, state):
            value = p_ref[g, pl.ds(i, SUB, stride=steps), :]
            return tuple(decay[r] * state[r] + value for r in range(modes))

        state = lax.fori_loop(0, steps, step, tuple(jnp.zeros((SUB, LANES), F32) for _ in range(modes)), unroll=8)
        for r in range(modes):
            v_ref[pl.ds(r * SUB, SUB), lanes] = state[r]
        return carry

    lax.fori_loop(0, groups, state_group, 0)

    go_halo.wait_recv()
    inner = jnp.where(s > 0, 1.0, 0.0).astype(F32)

    def first_group(g, carry):
        lanes = lane_group(g)
        prev = [rolled(halo[k, :, lanes].astype(F32) * inner) for k in range(3)]
        old = p_ref[g, pl.ds(0, SUB), :]
        filter_rows(g, lanes, load_taps(lanes), 0, prev)
        change = p_ref[g, pl.ds(0, SUB), :] - old
        change = [jnp.broadcast_to(change[k : k + 1], (SUB, LANES)) for k in (0, 1)]
        for r in range(modes):
            rate = row_of(rate_ref, r, lanes)
            far = jnp.exp(-rate * float(steps - 2))
            enter = far * (change[1] + jnp.exp(-rate) * change[0])
            total = v_ref[pl.ds(r * SUB, SUB), lanes] + jnp.where(place < 1, enter, 0.0)
            for n in (1, 2, 4):
                total = total + jnp.exp(-rate * float(n * steps)) * shifted(total, n)
            v_ref[pl.ds(r * SUB, SUB), lanes] = total
            s_own[pl.ds(r, 1), lanes] = total[SUB - 1 :]
        return carry

    lax.fori_loop(0, groups, first_group, 0)

    def conv_group(g, carry):
        lanes = lane_group(g)
        decay = [jnp.exp(-row_of(rate_ref, r, lanes)) for r in range(modes)]
        gain = [row_of(gain_ref, r, lanes) for r in range(modes)]
        enter = tuple(shifted(v_ref[pl.ds(r * SUB, SUB), lanes], 1) for r in range(modes))

        def step(i, state):
            at_step = pl.ds(i, SUB, stride=steps)
            value = p_ref[g, at_step, :]
            state = tuple(decay[r] * state[r] + value for r in range(modes))
            y_ref[g, at_step, :] = tree([gain[r] * state[r] for r in range(modes)])
            return state

        lax.fori_loop(0, steps, step, enter, unroll=8)
        return carry

    def tree(terms):
        while len(terms) > 1:
            terms = [terms[k] + terms[k + 1] for k in range(0, len(terms), 2)]
        return terms[0]

    swap = remote(s_own, s_sib, s_sem.at[0], s_sem.at[1], at(dcore=1))
    go(swap)
    lax.fori_loop(0, 1, conv_group, 0)
    swap.wait_recv()
    mine = pl.ds(pl.multiple_of(core * some, some), some)
    rate_half = rate_ref[mine, :]
    one = jnp.exp(-rate_half * float(toks))
    is_second = core == 1
    lead = jnp.where(is_second, s_sib[mine, :], s_own[mine, :])
    last = jnp.where(is_second, s_own[mine, :], s_sib[mine, :])
    t_buf[0] = one * lead + last
    for k in (1, 2, 3):
        go(remote(t_buf.at[0], t_buf.at[k], t_send.at[k], t_recv.at[k], at(dx=-BACK[k])))
    lax.fori_loop(1, 4, conv_group, 0)
    for k in (1, 2, 3):
        remote(t_buf.at[k], t_buf.at[k], t_send.at[k], t_recv.at[k], at(dcore=1)).wait_recv()

    unit = float(2 * toks)
    row = jnp.zeros((some, width), F32)
    for k in range(4):
        gap = (3 - ring(x, BACK[k])).astype(F32) * unit
        row = row + jnp.exp(-rate_half * gap) * t_buf[k]
    r_buf[0] = row
    onward = []
    for k in (1, 2, 3):
        copy = remote(r_buf.at[0], r_buf.at[k], r_send.at[k], r_recv.at[k], at(dz=-BACK[k]))
        later = ring(zh, -BACK[k]) > zh
        pl.when(later)(copy.start)
        onward.append((later, copy))
    w_from_x(0, 2, 1)
    w_z(0, (1,))
    w_from_z(1, 0)
    total = jnp.zeros((some, width), F32)
    for k in (1, 2, 3):
        other = ring(x, BACK[k])
        gap = jnp.maximum(x - 1 - other, 0).astype(F32) * unit
        total = total + jnp.where(other < x, jnp.exp(-rate_half * gap) * t_buf[k], 0.0)
    h_buf[mine, :] = total
    lax.fori_loop(4, 7, conv_group, 0)
    for k in (1, 2, 3):
        other = ring(zh, BACK[k])

        @pl.when(other < zh)
        def _():
            remote(r_buf.at[k], r_buf.at[k], r_send.at[k], r_recv.at[k], at(dcore=1)).wait_recv()
            gap = (4 * (zh - 1 - other) + x).astype(F32) * unit
            h_buf[mine, :] += jnp.exp(-rate_half * gap) * r_buf[k]

    share = remote(h_buf.at[mine], h_buf.at[mine], h_sem.at[0], h_sem.at[1], at(dcore=1))
    go(share)
    w_from_x(0, 1, 0)
    lax.fori_loop(7, 8, conv_group, 0)
    their = pl.ds(pl.multiple_of((1 - core) * some, some), some)
    remote(h_buf.at[their], h_buf.at[their], h_sem.at[0], h_sem.at[1], at(dcore=1)).wait_recv()

    def gate_group(g, carry):
        lanes = lane_group(g)
        decay, state = [], []
        for r in range(modes):
            rate = row_of(rate_ref, r, lanes)
            enter = row_of(h_buf, r, lanes)
            enter = jnp.where(is_second, jnp.exp(-rate * float(toks)) * enter + row_of(s_sib, r, lanes), enter)
            decay.append(jnp.exp(-rate * float(SUB)))
            state.append(row_of(gain_ref, r, lanes) * jnp.exp(-rate * (place + 1).astype(F32)) * enter)

        def step(m, state):
            rows = pl.ds(pl.multiple_of(m * 16, 16), 16)
            added = []
            for _ in (0, 1):
                added.append(tree(list(state)))
                state = tuple(decay[r] * state[r] for r in range(modes))
            conv = (y_ref[g, rows, :] + jnp.concatenate(added, axis=0)).astype(BF16).astype(F32)
            a_buf[c, rows, lanes] = (q_ref[rows, lanes] * conv).astype(BF16)
            return state

        lax.fori_loop(0, toks // 16, step, tuple(state), unroll=4)
        return carry

    lax.fori_loop(0, groups, gate_group, 0)

    def a_slot(dl, dy, part):
        first, count = PARTS[part]
        return a_buf.at[lax.rem(zl + dl, 2) * 4 + ring(y, BACK[dy]), pl.ds(first, count)]

    def a_y(dl, part):
        for way in (0, 1):
            go(remote(a_slot(dl, 0, part), a_slot(dl, 0, part), y_send.at[dl, part, way],
                      a_recv.at[dl, 1 + way, part], at(dy=(1, -1)[way])))

    def a_across(dy, part):
        go(remote(a_slot(0, dy, part), a_slot(0, dy, part), l_send.at[dy, part],
                  a_recv.at[1, dy, part], at(dl=1)))

    def a_wait(dl, dy, part):
        slot = a_slot(dl, dy, part)
        remote(slot, slot, l_send.at[dy, part], a_recv.at[dl, dy, part], at(dl=1)).wait_recv()

    def a_on(dl, dy, part):
        way = dy - 1
        go(remote(a_slot(dl, dy, part), a_slot(dl, dy, part), yf_send.at[dl, part],
                  a_recv.at[dl, 3, part], at(dy=(1, -1)[way])))

    def a_near(dl, part, dy):
        a_wait(dl, dy, part)
        if dy - 1 == part % 2:
            a_on(dl, dy, part)

    def multiply(stage):
        def ready(w_rank, a_rank, level):
            return jnp.logical_and(w_rank <= LEVELS[level][0], a_rank <= LEVELS[level][1])

        def block(ch, carry):
            dz = lax.rem(ch // 2 - zh + 4, 4)
            w_rank = jnp.where(dz == 0, 0, jnp.where(dz == 3, 1, jnp.where(dz == 1, 2, 3)))
            dy = lax.rem(lax.rem(ch, 4) - y + 4, 4)
            own = ch // 4 == zl
            a_rank = jnp.where(dy == 0, jnp.where(own, 0, 1), jnp.where(dy == 2, jnp.where(own, 3, 4), 2))
            now = ready(w_rank, a_rank, stage)
            if stage:
                now = jnp.logical_and(now, jnp.logical_not(ready(w_rank, a_rank, stage - 1)))

            @pl.when(now)
            def _():
                for n in range(0, width, 256):
                    acc[:, n : n + 256] += jnp.dot(a_buf[ch], w_buf[ch, :, n : n + 256],
                                                   preferred_element_type=F32)

            return carry

        lax.fori_loop(0, 8, block, 0)

    acc[...] = jnp.zeros_like(acc)
    keep.wait()
    w_from_z(2, 1)
    w_z(1, (0,))
    a_y(0, 0)
    w_from_z(2, 0)
    a_y(0, 3)
    w_from_x(1, 1, 0)
    w_from_z(3, 0)
    a_y(0, 2)
    w_x(3, 0, (1,))
    w_from_x(0, 3, 1)
    w_from_x(0, 3, 0)
    a_y(0, 1)
    a_across(0, 1)
    w_x(3, 0, (0,))
    a_near(0, 3, 2)
    w_from_x(0, 2, 0)
    w_from_x(2, 2, 1)
    a_near(0, 2, 1)
    w_from_z(3, 1)
    w_from_x(2, 1, 1)
    a_across(0, 0)
    w_x(3, 1, (0,))
    w_from_z(1, 1)
    a_wait(1, 0, 1)
    a_y(1, 1)
    w_from_x(2, 2, 0)
    a_near(0, 2, 2)
    w_from_x(3, 1, 0)
    a_across(0, 3)
    w_from_x(2, 1, 0)
    a_near(0, 3, 1)
    w_x(3, 1, (1,))
    w_from_x(1, 2, 1)
    a_across(2, 3)
    a_across(1, 3)
    a_across(0, 2)
    a_wait(1, 0, 0)
    a_y(1, 0)
    a_across(2, 2)
    w_from_x(3, 1, 1)
    a_near(0, 0, 1)
    w_from_x(3, 2, 1)
    a_near(1, 1, 1)
    a_wait(1, 0, 3)
    w_from_x(1, 2, 0)
    w_from_x(1, 3, 1)
    w_from_x(0, 1, 1)
    a_near(0, 1, 2)
    w_from_x(3, 2, 0)
    a_across(1, 2)
    w_from_x(2, 3, 1)
    w_from_x(2, 3, 0)
    w_from_x(3, 3, 0)
    w_from_x(1, 3, 0)
    a_wait(1, 1, 3)
    a_wait(1, 0, 2)
    a_wait(0, 3, 3)
    a_across(3, 3)
    a_near(1, 0, 2)
    w_whole(0)
    w_from_x(3, 3, 1)
    a_near(0, 1, 1)
    w_from_x(1, 1, 1)
    multiply(0)
    w_whole(1)
    w_whole(2)
    a_near(0, 0, 2)
    a_near(1, 0, 1)
    a_wait(0, 3, 2)
    a_across(3, 2)
    a_wait(1, 1, 2)
    a_wait(1, 2, 3)
    a_near(1, 1, 2)
    a_wait(1, 2, 2)
    multiply(1)
    w_whole(3)
    multiply(2)
    multiply(3)
    a_wait(1, 3, 3)
    a_wait(1, 3, 2)
    a_wait(0, 3, 0)
    a_wait(0, 3, 1)
    multiply(4)
    a_wait(1, 3, 1)
    a_wait(1, 3, 0)
    multiply(5)
    o_ref[...] = acc[...].astype(BF16)
    for copy in sent:
        copy.wait_send()
    for later, copy in onward:
        pl.when(later)(copy.wait_send)


def on_device(features, short_w, rates, residues, out_w):
    toks, _, width = features.shape
    modes = rates.shape[1]
    dma = pltpu.SemaphoreType.DMA
    vmem = pl.BlockSpec(memory_space=pltpu.VMEM)
    hbm = pl.BlockSpec(memory_space=pl.ANY)
    return pl.pallas_call(
        layer_kernel,
        out_shape=jax.ShapeDtypeStruct((toks, width), BF16),
        in_specs=[hbm, vmem, hbm, hbm, hbm],
        out_specs=vmem,
        scratch_shapes=[
            pltpu.VMEM((3, toks, width), BF16),
            pltpu.VMEM((8, 1024, width), BF16),
            pltpu.VMEM((8, toks, width), BF16),
            pltpu.VMEM((toks, width), F32),
            pltpu.VMEM((toks, width), F32),
            pltpu.VMEM((width // LANES, toks, LANES), F32),
            pltpu.VMEM((width // LANES, toks, LANES), F32),
            pltpu.VMEM((modes, width), F32),
            pltpu.VMEM((modes, width), F32),
            pltpu.VMEM((modes * SUB, width), F32),
            pltpu.VMEM((modes, width), F32),
            pltpu.VMEM((modes, width), F32),
            pltpu.VMEM((4, modes // 2, width), F32),
            pltpu.VMEM((4, modes // 2, width), F32),
            pltpu.VMEM((modes, width), F32),
            pltpu.VMEM((3, 16, width), BF16),
            dma, dma((2,)), dma((3,)), dma((2,)),
            dma((4, 2, 2)), dma((4, 2)), dma((2, 2)), dma((2,)), dma((4, 4, 2)), dma((4, 4, 2)), dma((4, 4, 2)),
            dma((2,)), dma((4,)), dma((4,)), dma((4,)), dma((4,)), dma((2,)),
            dma((2, 4, 2)), dma((2, 4)), dma((4, 4)), dma((2, 4, 4)),
        ],
        compiler_params=pltpu.CompilerParams(
            collective_id=0, has_side_effects=True, vmem_limit_bytes=60 * 2**20
        ),
    )(features.transpose(1, 0, 2), short_w, rates.T, residues.T, out_w)


def solution(mesh):
    in_specs = (P("seq", None, "ch"), P(None, None, "ch"), P(), P(), P("seq", "ch"))
    out_specs = P("seq", "ch")
    return jax.shard_map(
        on_device, mesh=mesh, in_specs=in_specs, out_specs=out_specs, check_vma=False
    )
```
